32 devices in a mesh: groups: 2 (over x), pts: 16 (over z, y, core).
Axes of the slice: x: 2, y: 2, z: 4, core: 2. Of those that a mesh axis runs over, the one named last changes fastest.
Arguments:
- points: bfloat16 [24576, 768], P(('groups', 'pts')), parts along dimension 0, may hold values from -6 to 6
- coverage: float32 [24576], P(('groups', 'pts')), parts along dimension 0, may hold values from 0 to 1.5
- candidates: bfloat16 [16384, 768], P(('groups', 'pts')), parts along dimension 0, may hold values from -0.21875 to 0.21875
- cand_mask: int32 [16384], P(('groups', 'pts')), parts along dimension 0, may hold values from 0 to 1, as said below
- send_block: int32 [32, 16], P(('groups', 'pts')), parts along dimension 0, may hold values from 0 to 3, as said below
- recv_src: int32 [32, 12], P(('groups', 'pts')), parts along dimension 0, may hold values from 0 to 15, as said below
- recv_block: int32 [32, 12], P(('groups', 'pts')), parts along dimension 0, may hold values from 0 to 3, as said below
- recv_live: int32 [32, 12], P(('groups', 'pts')), parts along dimension 0, may hold values from 0 to 1, as said below
Outputs:
- gains: float32 [16384], P(('groups', 'pts')), parts along dimension 0
The draws below stay inside these ranges and needn't reach their ends.
There are 2 independent parts, one for each index of `groups`. The reference program is written for one: setup_inputs(seed, part) draws one part's arguments, and reference() takes and returns one part's arrays. A program takes and returns all parts, laid end to end along the dimension named above; each array names one. Nothing has to cross between parts.
Inputs may be any that keep to these rules, and one draw needn't show every extreme that they name: Point shards 2 k to 2 k + 1 hold all points of cluster k. Every candidate block belongs to one cluster; a cluster has at most 12 blocks, some cluster exactly 12, and no device owns two blocks of one cluster. Padding rows (cand_mask 0) lie only at the end of a cluster's last block, fewer than half of it. send_block[d, p] is d's local block of the cluster of shard p when d owns one (exactly when d appears among p's live receive entries), else 0. `recv_src`: the live entries of row d come first and name each block of shard d's cluster once, so each owner at most once; dead entries name d itself. On live entries recv_block[d, r] equals send_block[recv_src[d, r], d]; dead entries are 0. `recv_live`: row d has as many live entries as its cluster has blocks; the rows of some shard are all live.
All inputs are finite; a program needn't handle non-finite values.
Results may differ from the reference program's by a relative error of at most 0.0003.
Values may be sent and summed in bfloat16 or wider, within the bound.
A program may use at most 128 MiB of HBM per device.

```python
import jax
import jax.numpy as jnp
from jax import lax

D = 768
PTS_DEV = 768
NB = 4
BLK = 128
SPAN = 2
RECV = 12
PTS = 12288
CANDS = 8192
N_PTS = 16


def layout(key):
    clusters = 8
    pairs = clusters // 2
    average = NB * SPAN
    offsets = jax.random.randint(jax.random.fold_in(key, 11), (pairs,), 0, average // 2 + 1)
    offsets = offsets.at[0].set(average // 2)
    counts = jnp.concatenate([average + offsets, average - offsets])
    order = jax.random.permutation(jax.random.fold_in(key, 12), clusters)
    counts = counts[order].astype(jnp.int32)
    ends = jnp.cumsum(counts).astype(jnp.int32)
    starts = ends - counts
    paddings = jax.random.randint(jax.random.fold_in(key, 13), (clusters,), 0, BLK // 2).astype(jnp.int32)
    return (counts, starts, ends, paddings)


def receive_lists(key):
    counts, starts, ends, paddings = layout(key)
    devices = jnp.arange(N_PTS, dtype=jnp.int32)
    cluster = devices // SPAN
    entries = jnp.arange(RECV, dtype=jnp.int32)
    global_ids = starts[cluster][:, None] + entries[None, :]
    living = entries[None, :] < counts[cluster][:, None]
    source = jnp.where(living, global_ids % N_PTS, devices[:, None])
    local = jnp.where(living, global_ids // N_PTS, 0)
    return (source.astype(jnp.int32), local.astype(jnp.int32), living.astype(jnp.int32))


def draw_recv_src(key, part):
    source, local, living = receive_lists(key)
    return source


def draw_recv_block(key, part):
    source, local, living = receive_lists(key)
    return local


def draw_recv_live(key, part):
    source, local, living = receive_lists(key)
    return living


def draw_send_block(key, part):
    counts, starts, ends, paddings = layout(key)
    owners = jnp.arange(N_PTS, dtype=jnp.int32)[:, None]
    cluster = jnp.arange(N_PTS, dtype=jnp.int32)[None, :] // SPAN
    first = starts[cluster]
    global_ids = first + jnp.mod(owners - first, N_PTS)
    living = global_ids < first + counts[cluster]
    return jnp.where(living, global_ids // N_PTS, 0).astype(jnp.int32)


def draw_cand_mask(key, part):
    counts, starts, ends, paddings = layout(key)
    owners = jnp.arange(N_PTS, dtype=jnp.int32)[:, None, None]
    locals_ = jnp.arange(NB, dtype=jnp.int32)[None, :, None]
    rows_in = jnp.arange(BLK, dtype=jnp.int32)[None, None, :]
    global_ids = locals_ * N_PTS + owners
    cluster = jnp.searchsorted(ends, global_ids, side='right').astype(jnp.int32)
    last_block = global_ids == ends[cluster] - 1
    padded = last_block & (rows_in >= BLK - paddings[cluster])
    return jnp.where(padded, 0, 1).astype(jnp.int32).reshape(-1)


def block_levels(key, extent, cuts, smallest, top_value):
    def one(dim, parts):
        steps = jax.random.uniform(jax.random.fold_in(jax.random.fold_in(key, 6), dim), (parts,), jnp.float32, smallest / len(cuts), top_value / len(cuts))
        return jnp.repeat(jnp.exp(steps), extent[dim] // parts).reshape((-1,) + (1,) * (len(extent) - dim - 1))

    factor_of = one(*cuts[0])
    for cut in cuts[1:]:
        factor_of = factor_of * one(*cut)
    return factor_of


def scatter_about(rng, shape, scale, reach, cuts=(), kind=jnp.bfloat16):
    loudness = block_levels(rng, shape, cuts, -0.22, 0.18) if cuts else 1.0
    values = jax.random.normal(rng, shape, jnp.float32) * scale * loudness
    return jnp.minimum(jnp.maximum(values, -reach), reach).astype(kind)


def setup_inputs(seed: int = 0, part: int = 0) -> dict:
    seeds = jax.random.split(jax.random.key(seed), 9)
    part_splits = jax.random.split(jax.random.fold_in(seeds[8], part), 9)
    return {
        "points": scatter_about(part_splits[0], (PTS, D), 1.0, 6.0, ((0, 16),)),
        "coverage": jnp.clip(1.5 * jax.random.uniform(part_splits[1], (PTS,), jnp.float32) ** block_levels(part_splits[1], (PTS,), ((0, 16),), -0.2, 0.2), 0.0, 1.5),
        "candidates": scatter_about(part_splits[2], (CANDS, D), D ** -0.5, 0.21875, ((0, 16),)),
        "cand_mask": draw_cand_mask(jax.random.fold_in(jax.random.fold_in(seeds[8], part), 71), part),
        "send_block": draw_send_block(jax.random.fold_in(jax.random.fold_in(seeds[8], part), 71), part),
        "recv_src": draw_recv_src(jax.random.fold_in(jax.random.fold_in(seeds[8], part), 71), part),
        "recv_block": draw_recv_block(jax.random.fold_in(jax.random.fold_in(seeds[8], part), 71), part),
        "recv_live": draw_recv_live(jax.random.fold_in(jax.random.fold_in(seeds[8], part), 71), part),
    }


def reference(points, coverage, candidates, cand_mask, send_block, recv_src, recv_block, recv_live):
    peers = N_PTS
    width = points.shape[1]
    shards = points.reshape(peers, PTS_DEV, width)
    levels = coverage.reshape(peers, PTS_DEV)
    blocks = candidates.reshape(peers, NB, BLK, width)
    devices = jnp.arange(peers, dtype=jnp.int32)
    sent = send_block[recv_src, devices[:, None]].astype(jnp.int32)

    def one_shard(items):
        shard, level, source, local, living = items
        chosen = blocks[source, local].astype(jnp.float32)
        scores = jnp.einsum('rcw,pw->rcp', chosen, shard.astype(jnp.float32))
        partial_value = jnp.sum(jnp.maximum(scores - level[None, None, :], 0.0), axis=2)
        return partial_value * living[:, None].astype(jnp.float32)

    partials = lax.map(one_shard, (shards, levels, recv_src, sent, recv_live))
    credit = (recv_src * NB + recv_block).reshape(-1).astype(jnp.int32)
    totals = jnp.zeros((peers * NB, BLK), jnp.float32).at[credit].add(partials.reshape(-1, BLK))
    return totals.reshape(-1) * cand_mask.astype(jnp.float32) / PTS_DEV
```

```python
import jax
import jax.numpy as jnp
from jax import lax
from jax.experimental import pallas as pl
from jax.experimental.pallas import tpu as pltpu
from jax.sharding import PartitionSpec as P

BLK = 128
LANES = 128
MESH = pl.DeviceIdType.MESH


def flipped(chip, step, chips):
    out = 0
    bit = 1
    while bit < chips:
        out = out + bit * ((chip // bit + step // bit) % 2)
        bit *= 2
    return out


def kernel(
    send_ref, src_ref, live_ref, points_ref, cov_ref, cand_ref, mask_ref, out_ref,
    inbox, stage, levels, living, part, ret,
    send_sem, recv_sem, give_sem, take_sem, back_sem, ret_sem,
):
    peers = ret.shape[0]
    chips = peers // 2
    owned = cand_ref.shape[0]
    shard_rows = points_ref.shape[0]
    me = lax.axis_index("pts")
    chip = me // 2
    core = me % 2
    sibling = chip * 2 + 1 - core

    barrier = pltpu.get_barrier_semaphore()

    def greet(s, _):
        pl.semaphore_signal(
            barrier, inc=1, device_id={"pts": (me + s) % peers}, device_id_type=MESH
        )
        return 0

    lax.fori_loop(1, peers, greet, 0)

    def pick(j, _):
        stage[j] = cand_ref[send_ref[0, 2 * j]]
        return 0

    lax.fori_loop(0, chips, pick, 0)

    def half(j, c):
        return inbox.at[j, pl.ds(pl.multiple_of(c * BLK, BLK), BLK), :]

    inbox[chip, pl.ds(pl.multiple_of(core * BLK, BLK), BLK), :] = cand_ref[send_ref[0, 2 * chip]]
    pl.semaphore_wait(barrier, peers - 1)

    def across(j, source):
        return pltpu.make_async_remote_copy(
            src_ref=stage.at[j],
            dst_ref=half(source, core),
            send_sem=send_sem.at[j],
            recv_sem=recv_sem.at[source],
            device_id={"pts": j * 2 + core},
            device_id_type=MESH,
        )

    def forward(j, c):
        return pltpu.make_async_remote_copy(
            src_ref=half(j, c),
            dst_ref=half(j, c),
            send_sem=give_sem.at[j],
            recv_sem=take_sem.at[j],
            device_id={"pts": sibling},
            device_id_type=MESH,
        )

    def give_back(owner, shard):
        return pltpu.make_async_remote_copy(
            src_ref=part.at[owner],
            dst_ref=ret.at[shard],
            send_sem=back_sem.at[owner],
            recv_sem=ret_sem.at[shard],
            device_id={"pts": owner},
            device_id_type=MESH,
        )

    def launch(t, _):
        across(flipped(chip, chips - t, chips), chip).start()
        return 0

    lax.fori_loop(1, chips, launch, 0)
    forward(chip, core).start()

    for i in range(shard_rows // LANES):
        row = cov_ref[pl.ds(i * LANES, LANES)].reshape(1, LANES)
        levels[pl.ds(i * LANES, LANES), :] = jnp.broadcast_to(row, (LANES, LANES)).T
    hits = (
        (lax.broadcasted_iota(jnp.int32, (peers, 1, src_ref.shape[1]), 0) == src_ref[...][None])
        & (live_ref[...][None] > 0)
    ).astype(jnp.float32)
    living[...] = jnp.broadcast_to(jnp.max(hits, axis=2, keepdims=True), living.shape)

    def score(j):
        forward(j, 1 - core).wait_recv()
        scores = lax.dot_general(
            points_ref[...], inbox[j], (((1,), (1,)), ((), ())),
            preferred_element_type=jnp.float32,
        )
        level = jnp.concatenate([levels[...], levels[...]], axis=1)
        sums = jnp.sum(jnp.maximum(scores - level, 0.0), axis=0, keepdims=True)
        part[2 * j] = sums[:, :BLK] * living[2 * j]
        part[2 * j + 1] = sums[:, BLK:] * living[2 * j + 1]

    def send_pair(j):
        give_back(2 * j, me).start()
        give_back(2 * j + 1, me).start()

    def arrive(j):
        across(chip, j).wait_recv()
        forward(j, core).start()

    arrive(flipped(chip, 1, chips))
    score(chip)
    ret[me] = part[me]
    give_back(sibling, me).start()

    def step(s, _):
        arrive(flipped(chip, s, chips))
        j = flipped(chip, s - 1, chips)
        score(j)
        send_pair(j)
        return 0

    lax.fori_loop(2, chips, step, 0)
    last = flipped(chip, chips - 1, chips)
    score(last)
    send_pair(last)

    def returned(s, _):
        give_back(me, (me + s) % peers).wait_recv()
        return 0

    lax.fori_loop(1, peers, returned, 0)

    def credit(p, total):
        slot = lax.broadcasted_iota(jnp.int32, (owned, BLK), 0)
        return total + jnp.where(slot == send_ref[0, p], ret[p], 0.0)

    total = lax.fori_loop(0, peers, credit, jnp.zeros((owned, BLK), jnp.float32))
    for b in range(owned):
        rows = pl.ds(b * BLK, BLK)
        out_ref[rows] = total[b] * mask_ref[rows].astype(jnp.float32) / shard_rows

    def drain_across(s, _):
        across(flipped(chip, s, chips), chip).wait_send()
        return 0

    lax.fori_loop(1, chips, drain_across, 0)

    def drain_forward(j, _):
        forward(j, core).wait_send()
        return 0

    lax.fori_loop(0, chips, drain_forward, 0)

    def drain_back(s, _):
        give_back((me + s) % peers, me).wait_send()
        return 0

    lax.fori_loop(1, peers, drain_back, 0)


def on_device(points, coverage, candidates, cand_mask, send_block, recv_src, recv_block, recv_live):
    peers = lax.axis_size("pts")
    chips = peers // 2
    rows, width = points.shape
    owned = candidates.shape[0] // BLK
    vmem = pl.BlockSpec(memory_space=pltpu.VMEM)
    block_bytes = BLK * width * 2
    need = (3 * chips + owned) * block_bytes + rows * width * 2 + rows * LANES * 4
    return pl.pallas_call(
        kernel,
        out_shape=jax.ShapeDtypeStruct((owned * BLK,), jnp.float32),
        in_specs=[pl.BlockSpec(memory_space=pltpu.SMEM)] + [vmem] * 6,
        out_specs=vmem,
        scratch_shapes=[
            pltpu.VMEM((chips, 2 * BLK, width), jnp.bfloat16),
            pltpu.VMEM((chips, BLK, width), jnp.bfloat16),
            pltpu.VMEM((rows, LANES), jnp.float32),
            pltpu.VMEM((peers, 1, LANES), jnp.float32),
            pltpu.VMEM((peers, 1, LANES), jnp.float32),
            pltpu.VMEM((peers, 1, LANES), jnp.float32),
            pltpu.SemaphoreType.DMA((chips,)),
            pltpu.SemaphoreType.DMA((chips,)),
            pltpu.SemaphoreType.DMA((chips,)),
            pltpu.SemaphoreType.DMA((chips,)),
            pltpu.SemaphoreType.DMA((peers,)),
            pltpu.SemaphoreType.DMA((peers,)),
        ],
        compiler_params=pltpu.CompilerParams(
            collective_id=0, has_side_effects=True, vmem_limit_bytes=need + (12 << 20)
        ),
    )(
        send_block, recv_src, recv_live, points, coverage,
        candidates.reshape(owned, BLK, width), cand_mask,
    )


def solution(mesh):
    return jax.shard_map(
        on_device,
        mesh=mesh,
        in_specs=(
            P(("groups", "pts"), None),
            P(("groups", "pts")),
            P(("groups", "pts"), None),
            P(("groups", "pts")),
            P(("groups", "pts"), None),
            P(("groups", "pts"), None),
            P(("groups", "pts"), None),
            P(("groups", "pts"), None),
        ),
        out_specs=P(("groups", "pts")),
        check_vma=False,
    )
```

```python
import jax
import jax.numpy as jnp
from jax import lax
from jax.experimental import pallas as pl
from jax.experimental.pallas import tpu as pltpu
from jax.sharding import PartitionSpec as P

BLK = 128
LANES = 128
MESH = pl.DeviceIdType.MESH


def flipped(chip, step, chips):
    out = 0
    bit = 1
    while bit < chips:
        out = out + bit * ((chip // bit + step // bit) % 2)
        bit *= 2
    return out


def kernel(
    send_hbm, src_hbm, live_hbm, points_hbm, cov_hbm, cand_hbm, mask_hbm, out_ref,
    send_ref, src_ref, live_ref, points_ref, cov_ref, cand_ref, mask_ref, fetch_sem, inbox, stage, levels, living, part, ret,
    send_sem, recv_sem, give_sem, take_sem, back_sem, ret_sem,
):
    peers = ret.shape[0]
    chips = peers // 2
    owned = cand_ref.shape[0]
    shard_rows = points_ref.shape[0]
    me = lax.axis_index("pts")
    chip = me // 2
    core = me % 2
    sibling = chip * 2 + 1 - core

    pairs = (
        (send_hbm, send_ref), (cand_hbm, cand_ref), (points_hbm, points_ref), (cov_hbm, cov_ref),
        (src_hbm, src_ref), (live_hbm, live_ref), (mask_hbm, mask_ref),
    )
    fetches = [
        pltpu.make_async_copy(far, near, fetch_sem.at[i]) for i, (far, near) in enumerate(pairs)
    ]
    for fetch in fetches:
        fetch.start()
    barrier = pltpu.get_barrier_semaphore()

    def greet(s, _):
        pl.semaphore_signal(
            barrier, inc=1, device_id={"pts": (me + s) % peers}, device_id_type=MESH
        )
        return 0

    lax.fori_loop(1, peers, greet, 0)

    fetches[0].wait()
    fetches[1].wait()

    def pick(j, _):
        stage[j] = cand_ref[send_ref[0, 2 * j]]
        return 0

    lax.fori_loop(0, chips, pick, 0)

    def half(j, c):
        return inbox.at[j, pl.ds(pl.multiple_of(c * BLK, BLK), BLK), :]

    inbox[chip, pl.ds(pl.multiple_of(core * BLK, BLK), BLK), :] = cand_ref[send_ref[0, 2 * chip]]
    pl.semaphore_wait(barrier, peers - 1)

    def across(j, source):
        return pltpu.make_async_remote_copy(
            src_ref=stage.at[j],
            dst_ref=half(source, core),
            send_sem=send_sem.at[j],
            recv_sem=recv_sem.at[source],
            device_id={"pts": j * 2 + core},
            device_id_type=MESH,
        )

    def forward(j, c):
        return pltpu.make_async_remote_copy(
            src_ref=half(j, c),
            dst_ref=half(j, c),
            send_sem=give_sem.at[j],
            recv_sem=take_sem.at[j],
            device_id={"pts": sibling},
            device_id_type=MESH,
        )

    def give_back(owner, shard):
        return pltpu.make_async_remote_copy(
            src_ref=part.at[owner],
            dst_ref=ret.at[shard],
            send_sem=back_sem.at[owner],
            recv_sem=ret_sem.at[shard],
            device_id={"pts": owner},
            device_id_type=MESH,
        )

    def launch(t, _):
        across(flipped(chip, t, chips), chip).start()
        return 0

    lax.fori_loop(1, chips, launch, 0)
    forward(chip, core).start()

    for fetch in fetches[2:]:
        fetch.wait()
    for i in range(shard_rows // LANES):
        row = cov_ref[pl.ds(i * LANES, LANES)].reshape(1, LANES)
        levels[pl.ds(i * LANES, LANES), :] = jnp.broadcast_to(row, (LANES, LANES)).T
    hits = (
        (lax.broadcasted_iota(jnp.int32, (peers, 1, src_ref.shape[1]), 0) == src_ref[...][None])
        & (live_ref[...][None] > 0)
    ).astype(jnp.float32)
    living[...] = jnp.broadcast_to(jnp.max(hits, axis=2, keepdims=True), living.shape)

    def score(j):
        forward(j, 1 - core).wait_recv()
        scores = lax.dot_general(
            points_ref[...], inbox[j], (((1,), (1,)), ((), ())),
            preferred_element_type=jnp.float32,
        )
        level = jnp.concatenate([levels[...], levels[...]], axis=1)
        sums = jnp.sum(jnp.maximum(scores - level, 0.0), axis=0, keepdims=True)
        part[2 * j] = sums[:, :BLK] * living[2 * j]
        part[2 * j + 1] = sums[:, BLK:] * living[2 * j + 1]

    def send_pair(j):
        give_back(2 * j, me).start()
        give_back(2 * j + 1, me).start()

    def arrive(j):
        across(chip, j).wait_recv()
        forward(j, core).start()

    arrive(flipped(chip, 1, chips))
    score(chip)
    ret[me] = part[me]
    give_back(sibling, me).start()

    def step(s, _):
        arrive(flipped(chip, s, chips))
        j = flipped(chip, s - 1, chips)
        score(j)
        send_pair(j)
        return 0

    lax.fori_loop(2, chips, step, 0)
    last = flipped(chip, chips - 1, chips)
    score(last)
    send_pair(last)

    def returned(s, _):
        give_back(me, (me + s) % peers).wait_recv()
        return 0

    lax.fori_loop(1, peers, returned, 0)

    def credit(p, total):
        slot = lax.broadcasted_iota(jnp.int32, (owned, BLK), 0)
        return total + jnp.where(slot == send_ref[0, p], ret[p], 0.0)

    total = lax.fori_loop(0, peers, credit, jnp.zeros((owned, BLK), jnp.float32))
    for b in range(owned):
        rows = pl.ds(b * BLK, BLK)
        out_ref[rows] = total[b] * mask_ref[rows].astype(jnp.float32) / shard_rows

    def drain_across(s, _):
        across(flipped(chip, s, chips), chip).wait_send()
        return 0

    lax.fori_loop(1, chips, drain_across, 0)

    def drain_forward(j, _):
        forward(j, core).wait_send()
        return 0

    lax.fori_loop(0, chips, drain_forward, 0)

    def drain_back(s, _):
        give_back((me + s) % peers, me).wait_send()
        return 0

    lax.fori_loop(1, peers, drain_back, 0)


def on_device(points, coverage, candidates, cand_mask, send_block, recv_src, recv_block, recv_live):
    peers = lax.axis_size("pts")
    chips = peers // 2
    rows, width = points.shape
    owned = candidates.shape[0] // BLK
    vmem = pl.BlockSpec(memory_space=pltpu.VMEM)
    block_bytes = BLK * width * 2
    need = (3 * chips + owned) * block_bytes + rows * width * 2 + rows * LANES * 4
    return pl.pallas_call(
        kernel,
        out_shape=jax.ShapeDtypeStruct((owned * BLK,), jnp.float32),
        in_specs=[pl.BlockSpec(memory_space=pltpu.HBM)] * 7,
        out_specs=vmem,
        scratch_shapes=[
            pltpu.SMEM(send_block.shape, jnp.int32),
            pltpu.VMEM(recv_src.shape, jnp.int32),
            pltpu.VMEM(recv_live.shape, jnp.int32),
            pltpu.VMEM(points.shape, points.dtype),
            pltpu.VMEM(coverage.shape, jnp.float32),
            pltpu.VMEM((owned, BLK, width), candidates.dtype),
            pltpu.VMEM(cand_mask.shape, jnp.int32),
            pltpu.SemaphoreType.DMA((7,)),
            pltpu.VMEM((chips, 2 * BLK, width), jnp.bfloat16),
            pltpu.VMEM((chips, BLK, width), jnp.bfloat16),
            pltpu.VMEM((rows, LANES), jnp.float32),
            pltpu.VMEM((peers, 1, LANES), jnp.float32),
            pltpu.VMEM((peers, 1, LANES), jnp.float32),
            pltpu.VMEM((peers, 1, LANES), jnp.float32),
            pltpu.SemaphoreType.DMA((chips,)),
            pltpu.SemaphoreType.DMA((chips,)),
            pltpu.SemaphoreType.DMA((chips,)),
            pltpu.SemaphoreType.DMA((chips,)),
            pltpu.SemaphoreType.DMA((peers,)),
            pltpu.SemaphoreType.DMA((peers,)),
        ],
        compiler_params=pltpu.CompilerParams(
            collective_id=0, has_side_effects=True, vmem_limit_bytes=need + (12 << 20)
        ),
    )(
        send_block, recv_src, recv_live, points, coverage,
        candidates.reshape(owned, BLK, width), cand_mask,
    )


def solution(mesh):
    return jax.shard_map(
        on_device,
        mesh=mesh,
        in_specs=(
            P(("groups", "pts"), None),
            P(("groups", "pts")),
            P(("groups", "pts"), None),
            P(("groups", "pts")),
            P(("groups", "pts"), None),
            P(("groups", "pts"), None),
            P(("groups", "pts"), None),
            P(("groups", "pts"), None),
        ),
        out_specs=P(("groups", "pts")),
        check_vma=False,
    )
```

```python
import jax
import jax.numpy as jnp
from jax import lax
from jax.experimental import pallas as pl
from jax.experimental.pallas import tpu as pltpu
from jax.sharding import PartitionSpec as P

BLK = 128
LANES = 128
MESH = pl.DeviceIdType.MESH


def flipped(chip, step, chips):
    out = 0
    bit = 1
    while bit < chips:
        out = out + bit * ((chip // bit + step // bit) % 2)
        bit *= 2
    return out


def kernel(
    send_hbm, src_hbm, live_hbm, points_hbm, cov_hbm, cand_hbm, mask_hbm, out_ref,
    send_ref, src_ref, live_ref, points_ref, cov_ref, cand_ref, mask_ref, fetch_sem, inbox, stage, levels, living, part, ret,
    send_sem, recv_sem, give_sem, take_sem, back_sem, ret_sem,
):
    peers = ret.shape[0]
    chips = peers // 2
    owned = cand_ref.shape[0]
    shard_rows = points_ref.shape[0]
    me = lax.axis_index("pts")
    chip = me // 2
    core = me % 2
    sibling = chip * 2 + 1 - core

    pairs = (
        (send_hbm, send_ref), (cand_hbm, cand_ref), (points_hbm, points_ref), (cov_hbm, cov_ref),
        (src_hbm, src_ref), (live_hbm, live_ref), (mask_hbm, mask_ref),
    )
    fetches = [
        pltpu.make_async_copy(far, near, fetch_sem.at[i]) for i, (far, near) in enumerate(pairs)
    ]
    for fetch in fetches[:2]:
        fetch.start()
    barrier = pltpu.get_barrier_semaphore()

    def greet(s, _):
        pl.semaphore_signal(
            barrier, inc=1, device_id={"pts": (me + s) % peers}, device_id_type=MESH
        )
        return 0

    lax.fori_loop(1, peers, greet, 0)

    fetches[0].wait()
    fetches[1].wait()
    for fetch in fetches[2:]:
        fetch.start()

    def pick(j, _):
        stage[j] = cand_ref[send_ref[0, 2 * j]]
        return 0

    lax.fori_loop(0, chips, pick, 0)

    def half(j, c):
        return inbox.at[j, pl.ds(pl.multiple_of(c * BLK, BLK), BLK), :]

    inbox[chip, pl.ds(pl.multiple_of(core * BLK, BLK), BLK), :] = cand_ref[send_ref[0, 2 * chip]]
    pl.semaphore_wait(barrier, peers - 1)

    def across(j, source):
        return pltpu.make_async_remote_copy(
            src_ref=stage.at[j],
            dst_ref=half(source, core),
            send_sem=send_sem.at[j],
            recv_sem=recv_sem.at[source],
            device_id={"pts": j * 2 + core},
            device_id_type=MESH,
        )

    def forward(j, c):
        return pltpu.make_async_remote_copy(
            src_ref=half(j, c),
            dst_ref=half(j, c),
            send_sem=give_sem.at[j],
            recv_sem=take_sem.at[j],
            device_id={"pts": sibling},
            device_id_type=MESH,
        )

    def give_back(owner, shard):
        return pltpu.make_async_remote_copy(
            src_ref=part.at[owner],
            dst_ref=ret.at[shard],
            send_sem=back_sem.at[owner],
            recv_sem=ret_sem.at[shard],
            device_id={"pts": owner},
            device_id_type=MESH,
        )

    def launch(t, _):
        across(flipped(chip, t, chips), chip).start()
        return 0

    lax.fori_loop(1, chips, launch, 0)
    forward(chip, core).start()

    for fetch in fetches[2:]:
        fetch.wait()
    for i in range(shard_rows // LANES):
        row = cov_ref[pl.ds(i * LANES, LANES)].reshape(1, LANES)
        levels[pl.ds(i * LANES, LANES), :] = jnp.broadcast_to(row, (LANES, LANES)).T
    hits = (
        (lax.broadcasted_iota(jnp.int32, (peers, 1, src_ref.shape[1]), 0) == src_ref[...][None])
        & (live_ref[...][None] > 0)
    ).astype(jnp.float32)
    living[...] = jnp.broadcast_to(jnp.max(hits, axis=2, keepdims=True), living.shape)

    def score(j):
        forward(j, 1 - core).wait_recv()
        scores = lax.dot_general(
            points_ref[...], inbox[j], (((1,), (1,)), ((), ())),
            preferred_element_type=jnp.float32,
        )
        level = jnp.concatenate([levels[...], levels[...]], axis=1)
        sums = jnp.sum(jnp.maximum(scores - level, 0.0), axis=0, keepdims=True)
        part[2 * j] = sums[:, :BLK] * living[2 * j]
        part[2 * j + 1] = sums[:, BLK:] * living[2 * j + 1]

    def arrive(j):
        across(chip, j).wait_recv()
        forward(j, core).start()

    def step(s, _):
        @pl.when(s < chips)
        def _():
            arrive(flipped(chip, s, chips))

        j = flipped(chip, s - 1, chips)
        score(j)

        @pl.when(s == 1)
        def _():
            ret[me] = part[me]
            give_back(sibling, me).start()

        @pl.when(s > 1)
        def _():
            give_back(2 * j, me).start()
            give_back(2 * j + 1, me).start()

        return 0

    lax.fori_loop(1, chips + 1, step, 0)

    def drain_across(s, _):
        across(flipped(chip, s, chips), chip).wait_send()
        return 0

    lax.fori_loop(1, chips, drain_across, 0)

    def drain_forward(j, _):
        forward(j, core).wait_send()
        return 0

    lax.fori_loop(0, chips, drain_forward, 0)

    def returned(s, _):
        give_back(me, (me + s) % peers).wait_recv()
        return 0

    lax.fori_loop(1, peers, returned, 0)

    def credit(p, total):
        slot = lax.broadcasted_iota(jnp.int32, (owned, BLK), 0)
        return total + jnp.where(slot == send_ref[0, p], ret[p], 0.0)

    total = lax.fori_loop(0, peers, credit, jnp.zeros((owned, BLK), jnp.float32))
    for b in range(owned):
        rows = pl.ds(b * BLK, BLK)
        out_ref[rows] = total[b] * mask_ref[rows].astype(jnp.float32) / shard_rows

    def drain_back(s, _):
        give_back((me + s) % peers, me).wait_send()
        return 0

    lax.fori_loop(1, peers, drain_back, 0)


def on_device(points, coverage, candidates, cand_mask, send_block, recv_src, recv_block, recv_live):
    peers = lax.axis_size("pts")
    chips = peers // 2
    rows, width = points.shape
    owned = candidates.shape[0] // BLK
    vmem = pl.BlockSpec(memory_space=pltpu.VMEM)
    block_bytes = BLK * width * 2
    need = (3 * chips + owned) * block_bytes + rows * width * 2 + rows * LANES * 4
    return pl.pallas_call(
        kernel,
        out_shape=jax.ShapeDtypeStruct((owned * BLK,), jnp.float32),
        in_specs=[pl.BlockSpec(memory_space=pltpu.HBM)] * 7,
        out_specs=vmem,
        scratch_shapes=[
            pltpu.SMEM(send_block.shape, jnp.int32),
            pltpu.VMEM(recv_src.shape, jnp.int32),
            pltpu.VMEM(recv_live.shape, jnp.int32),
            pltpu.VMEM(points.shape, points.dtype),
            pltpu.VMEM(coverage.shape, jnp.float32),
            pltpu.VMEM((owned, BLK, width), candidates.dtype),
            pltpu.VMEM(cand_mask.shape, jnp.int32),
            pltpu.SemaphoreType.DMA((7,)),
            pltpu.VMEM((chips, 2 * BLK, width), jnp.bfloat16),
            pltpu.VMEM((chips, BLK, width), jnp.bfloat16),
            pltpu.VMEM((rows, LANES), jnp.float32),
            pltpu.VMEM((peers, 1, LANES), jnp.float32),
            pltpu.VMEM((peers, 1, LANES), jnp.float32),
            pltpu.VMEM((peers, 1, LANES), jnp.float32),
            pltpu.SemaphoreType.DMA((chips,)),
            pltpu.SemaphoreType.DMA((chips,)),
            pltpu.SemaphoreType.DMA((chips,)),
            pltpu.SemaphoreType.DMA((chips,)),
            pltpu.SemaphoreType.DMA((peers,)),
            pltpu.SemaphoreType.DMA((peers,)),
        ],
        compiler_params=pltpu.CompilerParams(
            collective_id=0, has_side_effects=True, vmem_limit_bytes=max(need + (12 << 20), 60 << 20)
        ),
    )(
        send_block, recv_src, recv_live, points, coverage,
        candidates.reshape(owned, BLK, width), cand_mask,
    )


def solution(mesh):
    return jax.shard_map(
        on_device,
        mesh=mesh,
        in_specs=(
            P(("groups", "pts"), None),
            P(("groups", "pts")),
            P(("groups", "pts"), None),
            P(("groups", "pts")),
            P(("groups", "pts"), None),
            P(("groups", "pts"), None),
            P(("groups", "pts"), None),
            P(("groups", "pts"), None),
        ),
        out_specs=P(("groups", "pts")),
        check_vma=False,
    )
```

```python
import jax
import jax.numpy as jnp
from jax import lax
from jax.experimental import pallas as pl
from jax.experimental.pallas import tpu as pltpu
from jax.sharding import PartitionSpec as P

BLK = 128
LANES = 128
MESH = pl.DeviceIdType.MESH


def flipped(chip, step, chips):
    out = 0
    bit = 1
    while bit < chips:
        out = out + bit * ((chip // bit + step // bit) % 2)
        bit *= 2
    return out


def kernel(
    send_hbm, src_hbm, live_hbm, points_hbm, cov_hbm, cand_hbm, mask_hbm, out_ref,
    send_ref, src_ref, live_ref, points_ref, cov_ref, cand_ref, mask_ref, fetch_sem, inbox, stage, levels, living, part, ret,
    send_sem, recv_sem, give_sem, take_sem, back_sem, ret_sem,
):
    peers = ret.shape[0]
    chips = peers // 2
    owned = cand_ref.shape[0]
    shard_rows = points_ref.shape[0]
    me = lax.axis_index("pts")
    chip = me // 2
    core = me % 2
    sibling = chip * 2 + 1 - core

    pairs = (
        (send_hbm, send_ref), (cand_hbm, cand_ref), (points_hbm, points_ref), (cov_hbm, cov_ref),
        (src_hbm, src_ref), (live_hbm, live_ref), (mask_hbm, mask_ref),
    )
    fetches = [
        pltpu.make_async_copy(far, near, fetch_sem.at[i]) for i, (far, near) in enumerate(pairs)
    ]
    for fetch in fetches[:2]:
        fetch.start()
    barrier = pltpu.get_barrier_semaphore()

    def greet(s, _):
        pl.semaphore_signal(
            barrier, inc=1, device_id={"pts": (me + s) % peers}, device_id_type=MESH
        )
        return 0

    lax.fori_loop(1, peers, greet, 0)

    fetches[0].wait()
    fetches[1].wait()
    for fetch in fetches[2:]:
        fetch.start()

    def pick(j, _):
        stage[j] = cand_ref[send_ref[0, 2 * j]]
        return 0

    lax.fori_loop(0, chips, pick, 0)

    def half(j, c):
        return inbox.at[j, pl.ds(pl.multiple_of(c * BLK, BLK), BLK), :]

    inbox[chip, pl.ds(pl.multiple_of(core * BLK, BLK), BLK), :] = cand_ref[send_ref[0, 2 * chip]]
    pl.semaphore_wait(barrier, peers - 1)

    def across(j, source):
        return pltpu.make_async_remote_copy(
            src_ref=stage.at[j],
            dst_ref=half(source, core),
            send_sem=send_sem.at[j],
            recv_sem=recv_sem.at[source],
            device_id={"pts": j * 2 + core},
            device_id_type=MESH,
        )

    def forward(j, c):
        return pltpu.make_async_remote_copy(
            src_ref=half(j, c),
            dst_ref=half(j, c),
            send_sem=give_sem.at[j],
            recv_sem=take_sem.at[j],
            device_id={"pts": sibling},
            device_id_type=MESH,
        )

    def give_back(owner, shard):
        return pltpu.make_async_remote_copy(
            src_ref=part.at[owner],
            dst_ref=ret.at[shard],
            send_sem=back_sem.at[owner],
            recv_sem=ret_sem.at[shard],
            device_id={"pts": owner},
            device_id_type=MESH,
        )

    def launch(t, _):
        across(flipped(chip, t, chips), chip).start()
        return 0

    lax.fori_loop(1, chips, launch, 0)
    forward(chip, core).start()

    for fetch in fetches[2:]:
        fetch.wait()
    for i in range(shard_rows // LANES):
        row = cov_ref[pl.ds(i * LANES, LANES)].reshape(1, LANES)
        levels[pl.ds(i * LANES, LANES), :] = jnp.broadcast_to(row, (LANES, LANES)).T
    hits = (
        (lax.broadcasted_iota(jnp.int32, (peers, 1, src_ref.shape[1]), 0) == src_ref[...][None])
        & (live_ref[...][None] > 0)
    ).astype(jnp.float32)
    living[...] = jnp.broadcast_to(jnp.max(hits, axis=2, keepdims=True), living.shape)

    def score(j):
        forward(j, 1 - core).wait_recv()
        scores = lax.dot_general(
            points_ref[...], inbox[j], (((1,), (1,)), ((), ())),
            preferred_element_type=jnp.float32,
        )
        level = jnp.concatenate([levels[...], levels[...]], axis=1)
        sums = jnp.sum(jnp.maximum(scores - level, 0.0), axis=0, keepdims=True)
        part[2 * j] = sums[:, :BLK] * living[2 * j]
        part[2 * j + 1] = sums[:, BLK:] * living[2 * j + 1]

    def arrive(j):
        across(chip, j).wait_recv()
        forward(j, core).start()

    def step(s, _):
        @pl.when(s < chips)
        def _():
            arrive(flipped(chip, s, chips))

        j = flipped(chip, s - 1, chips)
        score(j)

        @pl.when(s == 1)
        def _():
            ret[me] = part[me]
            give_back(sibling, me).start()

        @pl.when(s > 1)
        def _():
            give_back(2 * j, me).start()
            give_back(2 * j + 1, me).start()

        return 0

    lax.fori_loop(1, chips + 1, step, 0)

    def drain_across(s, _):
        across(flipped(chip, s, chips), chip).wait_send()
        return 0

    lax.fori_loop(1, chips, drain_across, 0)

    def drain_forward(j, _):
        forward(j, core).wait_send()
        return 0

    lax.fori_loop(0, chips, drain_forward, 0)

    slot = lax.broadcasted_iota(jnp.int32, (owned, BLK), 0)

    def credit(p, total):
        return total + jnp.where(slot == send_ref[0, p], ret[p], 0.0)

    def returned(s, total):
        j = flipped(chip, s, chips)
        for p in (2 * j, 2 * j + 1):
            give_back(me, p).wait_recv()
            total = credit(p, total)
        return total

    give_back(me, sibling).wait_recv()
    total = credit(sibling, credit(me, jnp.zeros((owned, BLK), jnp.float32)))
    total = lax.fori_loop(1, chips, returned, total)
    for b in range(owned):
        rows = pl.ds(b * BLK, BLK)
        out_ref[rows] = total[b] * mask_ref[rows].astype(jnp.float32) / shard_rows

    def drain_back(s, _):
        give_back((me + s) % peers, me).wait_send()
        return 0

    lax.fori_loop(1, peers, drain_back, 0)


def on_device(points, coverage, candidates, cand_mask, send_block, recv_src, recv_block, recv_live):
    peers = lax.axis_size("pts")
    chips = peers // 2
    rows, width = points.shape
    owned = candidates.shape[0] // BLK
    vmem = pl.BlockSpec(memory_space=pltpu.VMEM)
    block_bytes = BLK * width * 2
    need = (3 * chips + owned) * block_bytes + rows * width * 2 + rows * LANES * 4
    return pl.pallas_call(
        kernel,
        out_shape=jax.ShapeDtypeStruct((owned * BLK,), jnp.float32),
        in_specs=[pl.BlockSpec(memory_space=pltpu.HBM)] * 7,
        out_specs=vmem,
        scratch_shapes=[
            pltpu.SMEM(send_block.shape, jnp.int32),
            pltpu.VMEM(recv_src.shape, jnp.int32),
            pltpu.VMEM(recv_live.shape, jnp.int32),
            pltpu.VMEM(points.shape, points.dtype),
            pltpu.VMEM(coverage.shape, jnp.float32),
            pltpu.VMEM((owned, BLK, width), candidates.dtype),
            pltpu.VMEM(cand_mask.shape, jnp.int32),
            pltpu.SemaphoreType.DMA((7,)),
            pltpu.VMEM((chips, 2 * BLK, width), jnp.bfloat16),
            pltpu.VMEM((chips, BLK, width), jnp.bfloat16),
            pltpu.VMEM((rows, LANES), jnp.float32),
            pltpu.VMEM((peers, 1, LANES), jnp.float32),
            pltpu.VMEM((peers, 1, LANES), jnp.float32),
            pltpu.VMEM((peers, 1, LANES), jnp.float32),
            pltpu.SemaphoreType.DMA((chips,)),
            pltpu.SemaphoreType.DMA((chips,)),
            pltpu.SemaphoreType.DMA((chips,)),
            pltpu.SemaphoreType.DMA((chips,)),
            pltpu.SemaphoreType.DMA((peers,)),
            pltpu.SemaphoreType.DMA((peers,)),
        ],
        compiler_params=pltpu.CompilerParams(
            collective_id=0, has_side_effects=True, vmem_limit_bytes=need + (12 << 20)
        ),
    )(
        *(
            pltpu.with_memory_space_constraint(x, pltpu.HBM)
            for x in (
                send_block, recv_src, recv_live, points, coverage,
                candidates.reshape(owned, BLK, width), cand_mask,
            )
        )
    )


def solution(mesh):
    return jax.shard_map(
        on_device,
        mesh=mesh,
        in_specs=(
            P(("groups", "pts"), None),
            P(("groups", "pts")),
            P(("groups", "pts"), None),
            P(("groups", "pts")),
            P(("groups", "pts"), None),
            P(("groups", "pts"), None),
            P(("groups", "pts"), None),
            P(("groups", "pts"), None),
        ),
        out_specs=P(("groups", "pts")),
        check_vma=False,
    )
```
